768 devices in a mesh: fsdp: 48 (over z, x_hi, core), rep: 16 (over x_lo, y).
Axes of the slice: x: 4 (x_hi: 2, x_lo: 2; x = x_hi * 2 + x_lo), y: 8, z: 12, core: 2. Of those that a mesh axis runs over, the one named last changes fastest.
Arguments:
- local_params: float32 [16, 18432, 1024], P('rep', 'fsdp'), may hold values from -400 to 400
- global_params: float32 [18432, 1024], P('fsdp'), may hold values from -6 to 6
- momentum: float32 [18432, 1024], P(('fsdp', 'rep')), may hold values from -4 to 4
Outputs:
- new_global: float32 [18432, 1024], P('fsdp')
- new_momentum: float32 [18432, 1024], P(('fsdp', 'rep'))
- mixed: float32 [16, 18432, 1024], P('rep', 'fsdp')
The draws below stay inside these ranges and needn't reach their ends.
All inputs are finite; a program needn't handle non-finite values.
Results may differ from the reference program's by a relative error of at most 0.005.
Values may be sent and summed in bfloat16 or wider, within the bound.
A program may use at most 32 MiB of HBM per device.

```python
import jax
import jax.numpy as jnp
from jax import lax

COLS = 1024
GROUP = 128
ROWS_DEV = 384
ROWS = 18432
REPS = 16


def shared_base(key):
    return jnp.clip(jax.random.normal(key, (ROWS, COLS), jnp.float32), -6.0, 6.0)


def draw_global_params(key, part):
    base = shared_base(key)
    return base


def draw_local_params(key, part):
    base = shared_base(key)
    key = jax.random.fold_in(key, 2)
    key_row = jax.random.fold_in(key, 0)
    key_col = jax.random.fold_in(key, 1)
    key_own = jax.random.fold_in(key, 3)
    row_scale = 10.0 ** jax.random.uniform(key_row, (ROWS, 1), jnp.float32)
    col_scale = 10.0 ** jax.random.uniform(key_col, (1, COLS), jnp.float32)
    row_ids = jnp.arange(ROWS, dtype=jnp.int32)
    shard_ids = (row_ids // ROWS_DEV).astype(jnp.float32)
    inside = (row_ids % ROWS_DEV).astype(jnp.float32)
    shard_count = max(ROWS // ROWS_DEV - 1, 1)
    ramp = (1.0 + 2.0 * shard_ids / shard_count) * (1.0 + 2.0 * inside / ROWS_DEV)
    ramp = ramp[:, None]
    noise = jnp.clip(jax.random.normal(key_own, (REPS, ROWS, COLS), jnp.float32), -4.0, 4.0)
    return base[None] + 0.1 * noise * (row_scale * col_scale * ramp)[None]


def level_of(rng, extent, cuts, smallest, largest):
    loudness, own = 1.0, jax.random.fold_in(rng, 6)
    for position, blocks in cuts:
        draws = jnp.exp(jax.random.uniform(jax.random.fold_in(own, position), (blocks,), jnp.float32, smallest / len(cuts), largest / len(cuts)))
        loudness = loudness * jnp.repeat(draws, extent[position] // blocks).reshape([-1 if axis == position else 1 for axis in range(len(extent))])
    return loudness


def bell_draw(stream_key, shape, scale, limit, shards=(), held_as=jnp.bfloat16):
    factor_of = level_of(stream_key, shape, shards, -0.22, 0.18) if shards else 1.0
    array = jax.random.normal(stream_key, shape, jnp.float32) * scale * factor_of
    return jnp.minimum(jnp.maximum(array, -limit), limit).astype(held_as)


def setup_inputs(seed: int = 0) -> dict:
    key_of = jax.random.split(jax.random.key(seed), 4)
    return {
        "local_params": draw_local_params(jax.random.fold_in(key_of[3], 71), 0),
        "global_params": draw_global_params(jax.random.fold_in(key_of[3], 71), 0),
        "momentum": bell_draw(key_of[2], (ROWS, COLS), 0.3, 4.0, ((0, 768),), jnp.float32),
    }


EPS = 1e-06
CLIP = 0.3
MU = 0.9
RATE = 0.7
MIXING = 0.5

def dequantized(delta):
    rows, cols = delta.shape
    groups = delta.reshape(rows, cols // GROUP, GROUP)
    scale = ((lax.optimization_barrier(jnp.max(jnp.abs(groups), axis=2)) + EPS) / 127.0).astype(jnp.bfloat16)
    wide_scale = scale.astype(jnp.float32)[:, :, None]
    coded = (groups / wide_scale).astype(jnp.bfloat16)
    return (coded.astype(jnp.float32) * wide_scale).reshape(rows, cols)

def reference(local_params, global_params, momentum):

    def accumulate(total, local):
        return (total + dequantized(global_params - local), None)
    start = jnp.zeros(global_params.shape, jnp.float32)
    summed, unused = lax.scan(accumulate, start, local_params)
    pseudo = summed / REPS
    rms = jnp.sqrt(jnp.sum(pseudo * pseudo) / (ROWS * COLS))
    factor = CLIP / jnp.maximum(rms, CLIP)
    clipped = pseudo * factor
    new_momentum = MU * momentum + clipped
    new_global = global_params - RATE * (clipped + MU * new_momentum)
    mixed = MIXING * new_global[None] + (1.0 - MIXING) * local_params
    return (new_global, new_momentum, mixed)
```

```python
import functools

import jax
import jax.numpy as jnp
from jax import lax
from jax.experimental import pallas as pl
from jax.experimental.pallas import tpu as pltpu
from jax.sharding import PartitionSpec as P

EPS = 1e-06
CLIP = 0.3
MU = 0.9
RATE = 0.7
MIXING = 0.5

MESH = pl.DeviceIdType.MESH
NY = 8
NXL = 2
NXH = 2
NZ = 12
REPS = NXL * NY
COLS = 1024
HALF = COLS // 2
SHARE = 24
BLK = 2 * SHARE
ROWS = SHARE * REPS
COUNT = float(ROWS * COLS * NZ * NXH * 2)
ORDER = (4, 3, 5, 2, 6, 1, 7, 0)


def fold(v):
    return jnp.concatenate([v[:, :HALF], v[:, HALF:]], axis=0)


def unfold(v):
    return jnp.concatenate([v[:SHARE], v[SHARE:]], axis=1)


def exchange(
    local_hbm, global_hbm, mom_hbm,
    pg, mg, pown, fout,
    lv, gv, mv, xs, xr, ys, yr, src, ary, arx, arz,
    load, rxs, rxr, rys, ryr, pys, pyr, pxs, pxr, mys, myr, mxs, mxr,
    ays, ayr, axs, axr, azs, azr,
):
    f = lax.axis_index("fsdp")
    r = lax.axis_index("rep")
    core = f % 2
    xh = (f // 2) % NXH
    z = f // (2 * NXH)
    a = r // NY
    y = r % NY
    other = 1 - a
    half_rows = ROWS // NXL

    def in_y(k):
        return a * NY + (y + k) % NY

    def y_dev(k):
        return (f, in_y(k))

    x_dev = (f, other * NY + y)

    loads = []
    for i, col in enumerate((other, a)):
        rows = pl.ds(pl.multiple_of(col * half_rows, 8), half_rows)
        for j, (s, d) in enumerate(((local_hbm, lv), (global_hbm, gv))):
            cp = pltpu.make_async_copy(s.at[rows], d.at[rows], load.at[2 * i + j])
            cp.start()
            loads.append(cp)
    mcp = pltpu.make_async_copy(mom_hbm, mv, load.at[4])
    mcp.start()

    ar_y = [y_dev(k) for k in range(1, NY)]
    ar_x = []
    for i in range(4):
        for j in range(2):
            if i or j:
                xx = (xh * 2 + a + i) % 4
                ar_x.append(((z * NXH + xx // 2) * 2 + (core + j) % 2, (xx % 2) * NY + y))
    ar_z = [((((z + k) % NZ) * NXH + xh) * 2 + core, r) for k in range(1, NZ)]
    barrier = pltpu.get_barrier_semaphore()
    partners = ar_y + ar_x + ar_z
    for d in partners:
        pl.semaphore_signal(barrier, inc=1, device_id=d, device_id_type=MESH)

    def remote(s, d, ss, rs, dev):
        return pltpu.make_async_remote_copy(
            src_ref=s, dst_ref=d, send_sem=ss, recv_sem=rs, device_id=dev, device_id_type=MESH
        )

    def delta(d):
        rows = pl.ds(pl.multiple_of(d * SHARE, 8), SHARE)
        return fold(gv[rows, :] - lv[rows, :])

    loads[0].wait()
    loads[1].wait()
    for k in ORDER:
        xs[k] = delta(other * NY + (y + k) % NY).astype(jnp.bfloat16)
    mcp.wait()
    mg[r] = fold(mv[...]).astype(jnp.bfloat16)

    pl.semaphore_wait(barrier, len(partners))

    sends = []

    def go(s, d, ss, rs, dev):
        cp = remote(s, d, ss, rs, dev)
        cp.start()
        sends.append(cp)
        return cp

    rx = {}
    for k in ORDER:
        rx[k] = go(xs.at[k], xr.at[k], rxs.at[k], rxr.at[k], x_dev)
    my = {}
    for k in (1, 7, 2, 6):
        my[k] = go(mg.at[r], mg.at[r], mys.at[k], myr.at[k], y_dev(k))
    loads[2].wait()
    loads[3].wait()
    ry = {}
    for k in ORDER:
        rx[k].wait_recv()
        v = delta(in_y(k)) + xr[k].astype(jnp.float32)
        if k:
            ys[k] = v.astype(jnp.bfloat16)
            ry[k] = go(ys.at[k], yr.at[k], rys.at[k], ryr.at[k], y_dev(k))
        else:
            total = v
    def got(arr, k):
        return arr.at[in_y(-k)]

    my[2].wait_recv()
    my[6].wait_recv()
    my[3] = go(got(mg, 2), got(mg, 2), mys.at[3], myr.at[3], y_dev(1))
    my[5] = go(got(mg, 6), got(mg, 6), mys.at[5], myr.at[5], y_dev(7))
    my[4] = go(got(mg, 2), got(mg, 2), mys.at[4], myr.at[4], y_dev(2))
    mx = {}
    mx[0] = go(mg.at[r], mg.at[r], mxs.at[0], mxr.at[0], x_dev)
    my[1].wait_recv()
    my[7].wait_recv()
    for k in (1, 7, 2, 6):
        mx[k] = go(got(mg, k), got(mg, k), mxs.at[k], mxr.at[k], x_dev)
    for k in (4, 3, 5, 2, 6, 1, 7):
        ry[k].wait_recv()
        total = total + yr[k].astype(jnp.float32)
    p = total * (1.0 / REPS)
    pown[...] = p
    sq = p * p
    sq = jnp.sum(sq, axis=0, keepdims=True)
    sq = sq[:, 0:128] + sq[:, 128:256] + sq[:, 256:384] + sq[:, 384:512]
    src[0] = sq
    ar = []
    for j, d in enumerate(ar_y):
        ar.append(go(src.at[0], ary.at[j], ays.at[j], ayr.at[j], d))
    pg[r] = p.astype(jnp.bfloat16)
    py = {}
    px = {}
    px[0] = go(pg.at[r], pg.at[r], pxs.at[0], pxr.at[0], x_dev)
    for k in (1, 7, 2, 6, 3, 5, 4):
        py[k] = go(pg.at[r], pg.at[r], pys.at[k], pyr.at[k], y_dev(k))

    def forward(ks):
        for k in ks:
            py[k].wait_recv()
            px[k] = go(got(pg, k), got(pg, k), pxs.at[k], pxr.at[k], x_dev)

    for cp in ar:
        cp.wait_recv()
    sq = sq + jnp.sum(ary[...], axis=0)
    src[1] = sq
    ar = []
    for j, d in enumerate(ar_x):
        ar.append(go(src.at[1], arx.at[j], axs.at[j], axr.at[j], d))
    forward((1, 7))
    for cp in ar:
        cp.wait_recv()
    sq = sq + jnp.sum(arx[...], axis=0)
    src[2] = sq
    ar = []
    for j, d in enumerate(ar_z):
        ar.append(go(src.at[2], arz.at[j], azs.at[j], azr.at[j], d))
    for k in (3, 5, 4):
        my[k].wait_recv()
        mx[k] = go(got(mg, k), got(mg, k), mxs.at[k], mxr.at[k], x_dev)
    forward((2, 6, 3, 5, 4))
    for cp in ar:
        cp.wait_recv()
    sq = sq + jnp.sum(arz[...], axis=0)
    rms = jnp.sqrt(jnp.sum(sq, axis=1, keepdims=True) * (1.0 / COUNT))
    fout[...] = jnp.broadcast_to(CLIP / jnp.maximum(rms, CLIP), fout.shape)
    for k in range(NY):
        mx[k].wait_recv()
        px[k].wait_recv()
    for cp in sends:
        cp.wait_send()


def finish(f_ref, pown, mom, pg, mg, local, glob, new_global, new_momentum, mixed):
    factor = f_ref[0:1, 0:1]
    g = glob.shape[0] // SHARE

    @pl.when(pl.program_id(0) == 0)
    def _():
        new_momentum[...] = MU * mom[...] + factor * unfold(pown[...])

    cp = factor * (RATE * (1.0 + MU))
    for i in range(g):
        rows = pl.ds(i * SHARE, SHARE)
        step = cp * pg[i].astype(jnp.float32) + (RATE * MU * MU) * mg[i].astype(jnp.float32)
        updated = glob[rows, :] - unfold(step)
        new_global[rows, :] = updated
        mixed[rows, :] = MIXING * updated + (1.0 - MIXING) * local[rows, :]


def shards(local_params, global_params, momentum):
    local = local_params[0]
    bf, f32 = jnp.bfloat16, jnp.float32
    vmem = pl.BlockSpec(memory_space=pltpu.VMEM)
    hbm = pl.BlockSpec(memory_space=pl.ANY)
    dma = pltpu.SemaphoreType.DMA
    gathered = jax.ShapeDtypeStruct((REPS, BLK, HALF), bf)
    pg, mg, pown, factor = pl.pallas_call(
        exchange,
        name="exchange",
        out_shape=[
            gathered,
            gathered,
            jax.ShapeDtypeStruct((BLK, HALF), f32),
            jax.ShapeDtypeStruct((8, 128), f32),
        ],
        in_specs=[hbm] * 3,
        out_specs=[vmem] * 4,
        scratch_shapes=[
            pltpu.VMEM((ROWS, COLS), f32),
            pltpu.VMEM((ROWS, COLS), f32),
            pltpu.VMEM((SHARE, COLS), f32),
            pltpu.VMEM((NY, BLK, HALF), bf),
            pltpu.VMEM((NY, BLK, HALF), bf),
            pltpu.VMEM((NY, BLK, HALF), bf),
            pltpu.VMEM((NY, BLK, HALF), bf),
            pltpu.VMEM((3, 1, 128), f32),
            pltpu.VMEM((NY - 1, 1, 128), f32),
            pltpu.VMEM((7, 1, 128), f32),
            pltpu.VMEM((NZ - 1, 1, 128), f32),
            dma((5,)),
        ]
        + [dma((NY,))] * 12
        + [dma((NY - 1,))] * 2
        + [dma((7,))] * 2
        + [dma((NZ - 1,))] * 2,
        compiler_params=pltpu.CompilerParams(
            collective_id=0, has_side_effects=True, vmem_limit_bytes=20 << 20
        ),
    )(local, global_params, momentum)

    steps = 4
    rows = ROWS // steps
    wide = pl.BlockSpec((rows, COLS), lambda i: (i, 0))
    blocks = pl.BlockSpec((REPS // steps, BLK, HALF), lambda i: (i, 0, 0))
    whole = lambda *s: pl.BlockSpec(s, lambda i: (0,) * len(s))
    new_global, new_momentum, mixed = pl.pallas_call(
        finish,
        name="finish",
        grid=(steps,),
        out_shape=[
            jax.ShapeDtypeStruct((ROWS, COLS), f32),
            jax.ShapeDtypeStruct((SHARE, COLS), f32),
            jax.ShapeDtypeStruct((ROWS, COLS), f32),
        ],
        in_specs=[whole(8, 128), whole(BLK, HALF), whole(SHARE, COLS), blocks, blocks, wide, wide],
        out_specs=[wide, whole(SHARE, COLS), wide],
        compiler_params=pltpu.CompilerParams(vmem_limit_bytes=16 << 20),
    )(factor, pown, momentum, pg, mg, local, global_params)
    return (new_global, new_momentum, mixed[None])


def solution(mesh):
    placed = (P("rep", "fsdp", None), P("fsdp", None), P(("fsdp", "rep"), None))
    return jax.shard_map(
        shards,
        mesh=mesh,
        in_specs=placed,
        out_specs=(P("fsdp", None), P(("fsdp", "rep"), None), P("rep", "fsdp", None)),
        check_vma=False,
    )
```

```python
import functools

import jax
import jax.numpy as jnp
from jax import lax
from jax.experimental import pallas as pl
from jax.experimental.pallas import tpu as pltpu
from jax.sharding import PartitionSpec as P

EPS = 1e-06
CLIP = 0.3
MU = 0.9
RATE = 0.7
MIXING = 0.5

MESH = pl.DeviceIdType.MESH
NY = 8
NXL = 2
NXH = 2
NX = NXL * NXH
NZ = 12
REPS = NXL * NY
COLS = 1024
HALF = COLS // 2
SHARE = 24
BLK = 2 * SHARE
ROWS = SHARE * REPS
COUNT = float(ROWS * COLS * NZ * NXH * 2)
N_XY = NX * NY - 1
N_ZC = 2 * NZ - 1
ORDER = (4, 3, 5, 2, 6, 1, 7, 0)


def fold(v):
    return jnp.concatenate([v[:, :HALF], v[:, HALF:]], axis=0)


def exchange(
    local_hbm, global_hbm, mom_hbm,
    pg, mg, pown, fout,
    lv, gv, mv, xs, xr, ys, yr, src, arxy, arzc,
    load, ssem, rxr, ryr, pyr, pxr, pnr, myr, mxr, asr, up,
):
    bf, f32 = jnp.bfloat16, jnp.float32
    f = lax.axis_index("fsdp")
    r = lax.axis_index("rep")
    core = f % 2
    xh = (f // 2) % NXH
    z = f // (2 * NXH)
    a = r // NY
    y = r % NY

    def wrap(t, n):
        return jnp.where(t >= n, t - n, t)

    yy = [y] + [wrap(y + k, NY) for k in range(1, NY)]
    col, ocol = a * NY, NY - a * NY
    own = [col + v for v in yy]
    oth = [ocol + v for v in yy]
    x_dev = (f, oth[0])

    def y_dev(k):
        return (f, own[k])

    loads = []
    half_rows = ROWS // NXL
    for i, c in enumerate((ocol, col)):
        rows = pl.ds(pl.multiple_of(c * SHARE, 8), half_rows)
        for j, (s, d) in enumerate(((local_hbm, lv), (global_hbm, gv))):
            cp = pltpu.make_async_copy(s.at[rows], d.at[rows], load.at[2 * i + j])
            cp.start()
            loads.append(cp)
    mcp = pltpu.make_async_copy(mom_hbm, mv, load.at[4])
    mcp.start()

    def far(steps, n):
        return min(steps, n - steps)

    xx = [xh * NXL + a] + [wrap(xh * NXL + a + i, NX) for i in range(1, NX)]
    fx = [z * (2 * NXH) + core + (v // NXL) * 2 for v in xx]
    rx0 = [(v % NXL) * NY for v in xx]
    near = sorted(((far(i, NX) + far(k, NY), i, k) for i in range(NX) for k in range(NY) if i or k), reverse=True)
    ar_xy = [(fx[i], rx0[i] + yy[k]) for _, i, k in near]
    def plane(zt, c):
        return ((zt * NXH + xh) * 2 + c, r)

    def to_planes(test, what):
        for zt in range(NZ):
            pl.when(test(zt))(functools.partial(what, zt))

    barrier = pltpu.get_barrier_semaphore()
    for d in ar_xy + [plane(z, 1 - core)]:
        pl.semaphore_signal(barrier, inc=1, device_id=d, device_id_type=MESH)

    def announce(sem, zt):
        for c in range(2):
            pl.semaphore_signal(sem, inc=1, device_id=plane(zt, c), device_id_type=MESH)

    to_planes(lambda zt: zt > z, functools.partial(announce, barrier))

    def remote(s, d, ss, rs, dev):
        return pltpu.make_async_remote_copy(
            src_ref=s, dst_ref=d, send_sem=ss, recv_sem=rs, device_id=dev, device_id_type=MESH
        )

    sent = {}

    def go(s, d, flow, rs, dev):
        cp = remote(s, d, ssem.at[flow], rs, dev)
        cp.start()
        sent[flow] = sent.get(flow, 0) + 1
        return cp

    def drain(flow):
        q = pg.at[pl.ds(0, sent[flow])]
        remote(q, q, ssem.at[flow], ssem.at[flow], x_dev).wait_send()

    seen = set()

    def arrived(cp):
        if id(cp) not in seen:
            seen.add(id(cp))
            cp.wait_recv()

    def delta(d):
        rows = pl.ds(pl.multiple_of(d * SHARE, 8), SHARE)
        return fold(gv[rows, :] - lv[rows, :])

    loads[0].wait()
    loads[1].wait()
    for k in ORDER:
        xs[k] = delta(oth[k]).astype(bf)
    pl.semaphore_wait(barrier, N_XY + 1 + 2 * z)

    def slot(buf, k):
        return buf.at[own[(NY - k) % NY]]

    def first(buf, flow, sems):
        return {k: go(buf.at[r], buf.at[r], flow, sems.at[k], y_dev(k)) for k in (2, 6, 1, 7)}

    def second(buf, flow, sems, got):
        arrived(got[2])
        got[3] = go(slot(buf, 2), slot(buf, 2), flow, sems.at[3], y_dev(1))
        arrived(got[6])
        got[5] = go(slot(buf, 6), slot(buf, 6), flow, sems.at[5], y_dev(7))
        s = buf.at[jnp.where(core == 0, own[6], own[2])]
        got[4] = go(s, s, flow, sems.at[4], (f, jnp.where(core == 0, own[2], own[6])))

    def over(buf, flow, sems, got, ks):
        res = {}
        for k in ks:
            if k:
                arrived(got[k])
            res[k] = go(slot(buf, k), slot(buf, k), flow, sems.at[k], x_dev)
        return res

    rx = {k: go(xs.at[k], xr.at[k], 0, rxr.at[k], x_dev) for k in ORDER}
    mcp.wait()
    mg[r] = fold(mv[...]).astype(bf)
    my = first(mg, 4, myr)
    to_planes(lambda zt: zt < z, functools.partial(announce, up))
    loads[2].wait()
    loads[3].wait()
    ry = {}
    for k in ORDER:
        rx[k].wait_recv()
        v = delta(own[k]) + xr[k].astype(f32)
        if k:
            ys[k] = v.astype(bf)
            ry[k] = go(ys.at[k], yr.at[k], 1, ryr.at[k], y_dev(k))
        else:
            total = v
    mx = over(mg, 5, mxr, my, (0, 1, 7, 2, 6))
    for k in ORDER[:-1]:
        ry[k].wait_recv()
        total = total + yr[k].astype(f32)
    p = total * (1.0 / REPS)
    sq = jnp.sum(p * p, axis=0, keepdims=True)
    sq = sq[:, 0:128] + sq[:, 128:256] + sq[:, 256:384] + sq[:, 384:512]
    src[0] = sq
    for j, d in enumerate(ar_xy):
        remote(src.at[0], arxy.at[j], asr.at[0], asr.at[1], d).start()

    pown[...] = p
    pg[r] = p.astype(bf)

    px = over(pg, 3, pxr, None, (0,))
    py = first(pg, 2, pyr)
    second(mg, 4, myr, my)

    pltpu.make_async_copy(arxy, arxy, asr.at[1]).wait()
    sq = sq + jnp.sum(arxy[...], axis=0)
    src[1] = sq
    mine = 2 * z + core
    arzc[mine] = sq

    def share(zt, c):
        remote(src.at[1], arzc.at[mine], asr.at[2], asr.at[3], plane(zt, c)).start()

    def share_both(zt):
        for c in range(2):
            share(zt, c)

    to_planes(lambda zt: zt < z, share_both)
    share(z, 1 - core)

    @pl.when(z < NZ - 1)
    def _():
        pl.semaphore_wait(up, 2 * (NZ - 1 - z))

    to_planes(lambda zt: zt > z, share_both)

    arrived(px[0])
    q = pg.at[oth[0]]
    pn = [go(q, q, 2, pnr.at[i], y_dev(k)) for i, k in enumerate((1, 7))]
    second(pg, 2, pyr, py)
    px.update(over(pg, 3, pxr, py, (2, 6)))
    mx.update(over(mg, 5, mxr, my, (3, 5, 4)))
    px.update(over(pg, 3, pxr, py, (3, 5, 4)))
    for cp in [py[1], py[7]] + pn + list(px.values()) + list(mx.values()):
        arrived(cp)
    for flow in range(6):
        drain(flow)
    remote(arxy, arxy, asr.at[0], asr.at[0], x_dev).wait_send()
    others = arzc.at[pl.ds(0, N_ZC)]
    remote(others, others, asr.at[2], asr.at[2], x_dev).wait_send()

    pltpu.make_async_copy(others, others, asr.at[3]).wait()
    sq = jnp.sum(arzc[...], axis=0)
    rms = jnp.sqrt(jnp.sum(sq, axis=1, keepdims=True) * (1.0 / COUNT))
    fout[...] = jnp.broadcast_to(CLIP / jnp.maximum(rms, CLIP), fout.shape)


def finish(f_ref, pown, mom, pg, mg, local, glob, new_global, new_momentum, mixed):
    factor = f_ref[0:1, 0:1]
    halves = [(0, pl.ds(0, HALF)), (SHARE, pl.ds(HALF, HALF))]

    @pl.when(pl.program_id(0) == 0)
    def _():
        for top, cols in halves:
            new_momentum[:, cols] = MU * mom[:, cols] + factor * pown[top:top + SHARE]

    cp = factor * (RATE * (1.0 + MU))
    for b in range(glob.shape[0] // SHARE):
        rows = pl.ds(b * SHARE, SHARE)
        step = cp * pg[b].astype(jnp.float32) + (RATE * MU * MU) * mg[b].astype(jnp.float32)
        for top, cols in halves:
            updated = glob[rows, cols] - step[top:top + SHARE]
            new_global[rows, cols] = updated
            mixed[rows, cols] = MIXING * updated + (1.0 - MIXING) * local[rows, cols]


def shards(local_params, global_params, momentum):
    local = local_params[0]
    bf, f32 = jnp.bfloat16, jnp.float32
    vmem = pl.BlockSpec(memory_space=pltpu.VMEM)
    hbm = pl.BlockSpec(memory_space=pltpu.HBM)
    dma = pltpu.SemaphoreType.DMA
    gathered = jax.ShapeDtypeStruct((REPS, BLK, HALF), bf)
    in_hbm = [pltpu.with_memory_space_constraint(v, pltpu.HBM) for v in (local, global_params, momentum)]
    pg, mg, pown, factor = pl.pallas_call(
        exchange,
        name="exchange",
        out_shape=[
            gathered,
            gathered,
            jax.ShapeDtypeStruct((BLK, HALF), f32),
            jax.ShapeDtypeStruct((8, 128), f32),
        ],
        in_specs=[hbm] * 3,
        out_specs=[vmem] * 4,
        scratch_shapes=[
            pltpu.VMEM((ROWS, COLS), f32),
            pltpu.VMEM((ROWS, COLS), f32),
            pltpu.VMEM((SHARE, COLS), f32),
        ]
        + [pltpu.VMEM((NY, BLK, HALF), bf)] * 4
        + [
            pltpu.VMEM((2, 1, 128), f32),
            pltpu.VMEM((N_XY, 1, 128), f32),
            pltpu.VMEM((N_ZC + 1, 1, 128), f32),
            dma((5,)),
            dma((6,)),
            dma((NY,)),
            dma((NY,)),
            dma((NY,)),
            dma((NY,)),
            dma((2,)),
            dma((NY,)),
            dma((NY,)),
            dma((4,)),
            pltpu.SemaphoreType.REGULAR,
        ],
        compiler_params=pltpu.CompilerParams(
            collective_id=0, has_side_effects=True, vmem_limit_bytes=20 << 20
        ),
    )(*in_hbm)

    steps = 4
    wide = pl.BlockSpec((ROWS // steps, COLS), lambda i: (i, 0))
    blocks = pl.BlockSpec((REPS // steps, BLK, HALF), lambda i: (i, 0, 0))

    def whole(*s):
        return pl.BlockSpec(s, lambda i: (0,) * len(s))

    new_global, new_momentum, mixed = pl.pallas_call(
        finish,
        name="finish",
        grid=(steps,),
        out_shape=[
            jax.ShapeDtypeStruct((ROWS, COLS), f32),
            jax.ShapeDtypeStruct((SHARE, COLS), f32),
            jax.ShapeDtypeStruct((ROWS, COLS), f32),
        ],
        in_specs=[whole(8, 128), whole(BLK, HALF), whole(SHARE, COLS), blocks, blocks, wide, wide],
        out_specs=[wide, whole(SHARE, COLS), wide],
        compiler_params=pltpu.CompilerParams(vmem_limit_bytes=16 << 20),
    )(factor, pown, momentum, pg, mg, local, global_params)
    return (new_global, new_momentum, mixed[None])


def solution(mesh):
    placed = (P("rep", "fsdp", None), P("fsdp", None), P(("fsdp", "rep"), None))
    return jax.shard_map(
        shards,
        mesh=mesh,
        in_specs=placed,
        out_specs=(P("fsdp", None), P(("fsdp", "rep"), None), P("rep", "fsdp", None)),
        check_vma=False,
    )
```

```python
import functools

import jax
import jax.numpy as jnp
from jax import lax
from jax.experimental import pallas as pl
from jax.experimental.pallas import tpu as pltpu
from jax.sharding import PartitionSpec as P

EPS = 1e-06
CLIP = 0.3
MU = 0.9
RATE = 0.7
MIXING = 0.5

MESH = pl.DeviceIdType.MESH
NY = 8
NXL = 2
NXH = 2
NX = NXL * NXH
NZ = 12
REPS = NXL * NY
COLS = 1024
HALF = COLS // 2
SHARE = 24
BLK = 2 * SHARE
ROWS = SHARE * REPS
COUNT = float(ROWS * COLS * NZ * NXH * 2)
N_XY = NX * NY - 1
N_ZC = 2 * NZ - 1
STEPS = 4
ORDER = (3, 5, 2, 6, 1, 7)
FAR = NY // 2


def fold(v):
    return jnp.concatenate([v[:, :HALF], v[:, HALF:]], axis=0)


def exchange(
    local_hbm, global_hbm, mom_hbm,
    pg, mg, pown, fout,
    lv, gv, mv, xs, xr, ys, yr, fs, fr, src, arxy, arzc,
    load, ssem, rxr, ryr, far_sem, pyr, pxr, pnr, myr, mxr, asr, up, hop, pair, side, both,
):
    bf, f32 = jnp.bfloat16, jnp.float32
    f = lax.axis_index("fsdp")
    r = lax.axis_index("rep")
    core = f % 2
    xh = (f // 2) % NXH
    z = f // (2 * NXH)
    a = r // NY
    y = r % NY

    def wrap(t, n):
        return jnp.where(t >= n, t - n, t)

    yy = [y] + [wrap(y + k, NY) for k in range(1, NY)]
    col, ocol = a * NY, NY - a * NY
    own = [col + v for v in yy]
    oth = [ocol + v for v in yy]
    x_dev = (f, oth[0])

    def y_dev(k):
        return (f, own[k])

    loads = []
    half_rows = ROWS // NXL
    for i, c in enumerate((ocol, col)):
        rows = pl.ds(pl.multiple_of(c * SHARE, 8), half_rows)
        for j, (s, d) in enumerate(((local_hbm, lv), (global_hbm, gv))):
            cp = pltpu.make_async_copy(s.at[rows], d.at[rows], load.at[2 * i + j])
            cp.start()
            loads.append(cp)
    mcp = pltpu.make_async_copy(mom_hbm, mv, load.at[4])
    mcp.start()

    def far(steps, n):
        return min(steps, n - steps)

    xx = [xh * NXL + a] + [wrap(xh * NXL + a + i, NX) for i in range(1, NX)]
    fx = [z * (2 * NXH) + core + (v // NXL) * 2 for v in xx]
    rx0 = [(v % NXL) * NY for v in xx]
    near = sorted(((far(i, NX) + far(k, NY), i, k) for i in range(NX) for k in range(NY) if i or k), reverse=True)
    ar_xy = [(fx[i], rx0[i] + yy[k]) for _, i, k in near]
    def plane(zt, c):
        return ((zt * NXH + xh) * 2 + c, r)

    def to_planes(test, what):
        for zt in range(NZ):
            pl.when(test(zt))(functools.partial(what, zt))

    def tell(sem, d):
        pl.semaphore_signal(sem, inc=1, device_id=d, device_id_type=MESH)

    def announce(sem, zt):
        for c in range(2):
            tell(sem, plane(zt, c))

    beside = ((z * NXH + 1 - xh) * 2 + core, r)
    barrier = pltpu.get_barrier_semaphore()
    for d in (y_dev(FAR), x_dev, y_dev(1), y_dev(NY - 1), plane(z, 1 - core)):
        tell(barrier, d)

    @pl.when(xh == 0)
    def _():
        tell(barrier, beside)

    to_planes(lambda zt: zt > z, functools.partial(announce, barrier))

    def hop_out(level):
        tell(hop.at[level, 0], y_dev(1))
        tell(hop.at[level, 1], y_dev(NY - 1))

    def hop_in(level):
        pl.semaphore_wait(hop.at[level, 0], 1)
        pl.semaphore_wait(hop.at[level, 1], 1)

    def remote(s, d, ss, rs, dev):
        return pltpu.make_async_remote_copy(
            src_ref=s, dst_ref=d, send_sem=ss, recv_sem=rs, device_id=dev, device_id_type=MESH
        )

    sent = {}

    def go(s, d, flow, rs, dev):
        cp = remote(s, d, ssem.at[flow], rs, dev)
        cp.start()
        sent[flow] = sent.get(flow, 0) + 1
        return cp

    def drain(flow):
        q = pg.at[pl.ds(0, sent[flow])]
        remote(q, q, ssem.at[flow], ssem.at[flow], x_dev).wait_send()

    seen = set()

    def arrived(cp):
        if id(cp) not in seen:
            seen.add(id(cp))
            cp.wait_recv()

    def delta(d):
        rows = pl.ds(pl.multiple_of(d * SHARE, 8), SHARE)
        return fold(gv[rows, :] - lv[rows, :])

    loads[0].wait()
    loads[1].wait()
    fs[0] = delta(oth[FAR]).astype(bf)
    for k in ORDER:
        xs[k] = delta(oth[k]).astype(bf)
    pl.semaphore_wait(barrier, 5 + xh + 2 * z)

    def slot(buf, k):
        return buf.at[own[(NY - k) % NY]]

    def first(buf, flow, sems):
        return {k: go(buf.at[r], buf.at[r], flow, sems.at[k], y_dev(k)) for k in (2, 6, 1, 7)}

    def second(buf, flow, sems, got):
        arrived(got[2])
        got[3] = go(slot(buf, 2), slot(buf, 2), flow, sems.at[3], y_dev(1))
        arrived(got[6])
        got[5] = go(slot(buf, 6), slot(buf, 6), flow, sems.at[5], y_dev(7))
        s = buf.at[jnp.where(core == 0, own[6], own[2])]
        got[4] = go(s, s, flow, sems.at[4], (f, jnp.where(core == 0, own[2], own[6])))

    def over(buf, flow, sems, got, ks):
        res = {}
        for k in ks:
            if k:
                arrived(got[k])
            res[k] = go(slot(buf, k), slot(buf, k), flow, sems.at[k], x_dev)
        return res

    def send_far(i):
        return go(fs.at[i], fr.at[i], 6, far_sem.at[i], y_dev(FAR))

    hop_out(0)
    rf = [send_far(0)]
    rx = {k: go(xs.at[k], xr.at[k], 0, rxr.at[k], x_dev) for k in ORDER}
    loads[2].wait()
    loads[3].wait()
    fs[1] = delta(own[FAR]).astype(bf)
    rf.append(send_far(1))
    hop_in(0)
    hop_out(1)

    @pl.when(xh == 1)
    def _():
        tell(side, beside)

    mcp.wait()
    mg[r] = fold(mv[...]).astype(bf)
    hop_in(1)
    tell(pair, x_dev)
    to_planes(lambda zt: zt < z, functools.partial(announce, up))
    ry = {}
    for k in ORDER:
        rx[k].wait_recv()
        ys[k] = (delta(own[k]) + xr[k].astype(f32)).astype(bf)
        ry[k] = go(ys.at[k], yr.at[k], 1, ryr.at[k], y_dev(k))
        if k == ORDER[2]:
            pl.semaphore_wait(pair, 1)

            @pl.when(xh == 0)
            def _():
                pl.semaphore_wait(side, 1)

            tell(both, beside)
    rf[0].wait_recv()
    xs[0] = (delta(oth[0]) + fr[0].astype(f32)).astype(bf)
    rx[0] = go(xs.at[0], xr.at[0], 0, rxr.at[0], x_dev)
    rf[1].wait_recv()
    total = delta(own[0]) + fr[1].astype(f32)
    for k in ORDER:
        ry[k].wait_recv()
        total = total + yr[k].astype(f32)
    rx[0].wait_recv()
    total = total + xr[0].astype(f32)
    p = total * (1.0 / REPS)
    sq = jnp.sum(p * p, axis=0, keepdims=True)
    sq = sq[:, 0:128] + sq[:, 128:256] + sq[:, 256:384] + sq[:, 384:512]
    src[0] = sq
    pl.semaphore_wait(both, 1)
    for j, d in enumerate(ar_xy):
        remote(src.at[0], arxy.at[j], asr.at[0], asr.at[1], d).start()

    pown[...] = p
    pg[r] = p.astype(bf)

    px = over(pg, 3, pxr, None, (0,))
    py = first(pg, 2, pyr)
    my = first(mg, 4, myr)
    mx = over(mg, 5, mxr, my, (0,))

    pltpu.make_async_copy(arxy, arxy, asr.at[1]).wait()
    sq = sq + jnp.sum(arxy[...], axis=0)
    src[1] = sq
    mine = 2 * z + core
    arzc[mine] = sq

    def share(zt, c):
        remote(src.at[1], arzc.at[mine], asr.at[2], asr.at[3], plane(zt, c)).start()

    def share_both(zt):
        for c in range(2):
            share(zt, c)

    to_planes(lambda zt: zt < z, share_both)
    share(z, 1 - core)

    @pl.when(z < NZ - 1)
    def _():
        pl.semaphore_wait(up, 2 * (NZ - 1 - z))

    to_planes(lambda zt: zt > z, share_both)

    arrived(px[0])
    q = pg.at[oth[0]]
    pn = [go(q, q, 2, pnr.at[i], y_dev(k)) for i, k in enumerate((1, 7))]
    second(pg, 2, pyr, py)
    px.update(over(pg, 3, pxr, py, (2, 6)))
    second(mg, 4, myr, my)
    mx.update(over(mg, 5, mxr, my, (2, 6, 1, 7)))
    px.update(over(pg, 3, pxr, py, (3, 5, 4)))
    mx.update(over(mg, 5, mxr, my, (3, 5, 4)))
    for cp in [py[1], py[7]] + pn + list(px.values()) + list(mx.values()):
        arrived(cp)
    for flow in range(7):
        drain(flow)
    remote(arxy, arxy, asr.at[0], asr.at[0], x_dev).wait_send()
    others = arzc.at[pl.ds(0, N_ZC)]
    remote(others, others, asr.at[2], asr.at[2], x_dev).wait_send()

    pltpu.make_async_copy(others, others, asr.at[3]).wait()
    sq = jnp.sum(arzc[...], axis=0)
    rms = jnp.sqrt(jnp.sum(sq, axis=1, keepdims=True) * (1.0 / COUNT))
    fout[...] = jnp.broadcast_to(CLIP / jnp.maximum(rms, CLIP), fout.shape)


def finish(f_ref, pown, mom, pg, mg, local, glob, new_global, new_momentum, mixed, gbuf, mbuf, xbuf, sem):
    factor = f_ref[0:1, 0:1]
    halves = [(0, pl.ds(0, HALF)), (SHARE, pl.ds(HALF, HALF))]
    cp = factor * (RATE * (1.0 + MU))
    copies = []
    per = REPS // STEPS
    for t in range(STEPS):
        for b in range(t * per, (t + 1) * per):
            rows = pl.ds(b * SHARE, SHARE)
            step = cp * pg[b].astype(jnp.float32) + (RATE * MU * MU) * mg[b].astype(jnp.float32)
            for top, cols in halves:
                updated = glob[rows, cols] - step[top:top + SHARE]
                gbuf[rows, cols] = updated
                xbuf[rows, cols] = MIXING * updated + (1.0 - MIXING) * local[rows, cols]
        rows = pl.ds(t * per * SHARE, per * SHARE)
        for i, (s, d) in enumerate(((gbuf, new_global), (xbuf, mixed))):
            q = pltpu.make_async_copy(s.at[rows], d.at[rows], sem.at[2 * t + i])
            q.start()
            copies.append(q)
    for top, cols in halves:
        mbuf[:, cols] = MU * mom[:, cols] + factor * pown[top:top + SHARE]
    q = pltpu.make_async_copy(mbuf, new_momentum, sem.at[2 * STEPS])
    q.start()
    copies.append(q)
    for q in copies:
        q.wait()


def shards(local_params, global_params, momentum):
    local = local_params[0]
    bf, f32 = jnp.bfloat16, jnp.float32
    vmem = pl.BlockSpec(memory_space=pltpu.VMEM)
    hbm = pl.BlockSpec(memory_space=pltpu.HBM)
    dma = pltpu.SemaphoreType.DMA
    gathered = jax.ShapeDtypeStruct((REPS, BLK, HALF), bf)
    in_hbm = [pltpu.with_memory_space_constraint(v, pltpu.HBM) for v in (local, global_params, momentum)]
    pg, mg, pown, factor = pl.pallas_call(
        exchange,
        name="exchange",
        out_shape=[
            gathered,
            gathered,
            jax.ShapeDtypeStruct((BLK, HALF), f32),
            jax.ShapeDtypeStruct((8, 128), f32),
        ],
        in_specs=[hbm] * 3,
        out_specs=[vmem] * 4,
        scratch_shapes=[
            pltpu.VMEM((ROWS, COLS), f32),
            pltpu.VMEM((ROWS, COLS), f32),
            pltpu.VMEM((SHARE, COLS), f32),
        ]
        + [pltpu.VMEM((NY, BLK, HALF), bf)] * 4
        + [pltpu.VMEM((2, BLK, HALF), bf)] * 2
        + [
            pltpu.VMEM((2, 1, 128), f32),
            pltpu.VMEM((N_XY, 1, 128), f32),
            pltpu.VMEM((N_ZC + 1, 1, 128), f32),
            dma((5,)),
            dma((7,)),
            dma((NY,)),
            dma((NY,)),
            dma((2,)),
            dma((NY,)),
            dma((NY,)),
            dma((2,)),
            dma((NY,)),
            dma((NY,)),
            dma((4,)),
            pltpu.SemaphoreType.REGULAR,
            pltpu.SemaphoreType.REGULAR((2, 2)),
            pltpu.SemaphoreType.REGULAR,
            pltpu.SemaphoreType.REGULAR,
            pltpu.SemaphoreType.REGULAR,
        ],
        compiler_params=pltpu.CompilerParams(
            collective_id=0, has_side_effects=True, vmem_limit_bytes=20 << 20
        ),
    )(*in_hbm)

    any_space = pl.BlockSpec(memory_space=pl.ANY)
    new_global, new_momentum, mixed = pl.pallas_call(
        finish,
        name="finish",
        out_shape=[
            jax.ShapeDtypeStruct((ROWS, COLS), f32),
            jax.ShapeDtypeStruct((SHARE, COLS), f32),
            jax.ShapeDtypeStruct((ROWS, COLS), f32),
        ],
        in_specs=[vmem] * 7,
        out_specs=[any_space] * 3,
        scratch_shapes=[
            pltpu.VMEM((ROWS, COLS), f32),
            pltpu.VMEM((SHARE, COLS), f32),
            pltpu.VMEM((ROWS, COLS), f32),
            dma((2 * STEPS + 1,)),
        ],
        compiler_params=pltpu.CompilerParams(vmem_limit_bytes=16 << 20),
    )(factor, pown, momentum, pg, mg, local, global_params)
    return (new_global, new_momentum, mixed[None])


def solution(mesh):
    placed = (P("rep", "fsdp", None), P("fsdp", None), P(("fsdp", "rep"), None))
    return jax.shard_map(
        shards,
        mesh=mesh,
        in_specs=placed,
        out_specs=(P("fsdp", None), P(("fsdp", "rep"), None), P("rep", "fsdp", None)),
        check_vma=False,
    )
```

```python
import functools

import jax
import jax.numpy as jnp
from jax import lax
from jax.experimental import pallas as pl
from jax.experimental.pallas import tpu as pltpu
from jax.sharding import PartitionSpec as P

EPS = 1e-06
CLIP = 0.3
MU = 0.9
RATE = 0.7
MIXING = 0.5

MESH = pl.DeviceIdType.MESH
NY = 8
NXL = 2
NXH = 2
NX = NXL * NXH
NZ = 12
REPS = NXL * NY
COLS = 1024
HALF = COLS // 2
SHARE = 24
BLK = 2 * SHARE
ROWS = SHARE * REPS
FIRST = 4
COUNT = float(ROWS * COLS * NZ * NXH * 2)
N_XY = NX * NY - 1
N_ZC = 2 * NZ - 1
STEPS = 4
ORDER = (3, 5, 2, 6, 1, 7)
FAR = NY // 2


def fold(v):
    return jnp.concatenate([v[:, :HALF], v[:, HALF:]], axis=0)


def exchange(
    local_hbm, global_hbm, mom_hbm,
    pg, mg, pown, fout, lv, gv, mv,
    xs, xr, ys, yr, fs, fr, src, arxy, arzc,
    load, ssem, rxr, ryr, far_sem, pyr, pxr, pnr, myr, mxr, mnr, asr, up, hop, pair, side, both,
):
    bf, f32 = jnp.bfloat16, jnp.float32
    f = lax.axis_index("fsdp")
    r = lax.axis_index("rep")
    core = f % 2
    xh = (f // 2) % NXH
    z = f // (2 * NXH)
    a = r // NY
    y = r % NY

    def wrap(t, n):
        return jnp.where(t >= n, t - n, t)

    yy = [y] + [wrap(y + k, NY) for k in range(1, NY)]
    col, ocol = a * NY, NY - a * NY
    own = [col + v for v in yy]
    oth = [ocol + v for v in yy]
    x_dev = (f, oth[0])

    def y_dev(k):
        return (f, own[k])

    loads = []
    half_rows = ROWS // NXL
    for i, c in enumerate((ocol, col)):
        rows = pl.ds(pl.multiple_of(c * SHARE, 8), half_rows)
        for j, (s, d) in enumerate(((local_hbm, lv), (global_hbm, gv))):
            cp = pltpu.make_async_copy(s.at[rows], d.at[rows], load.at[2 * i + j])
            cp.start()
            loads.append(cp)
    mcp = pltpu.make_async_copy(mom_hbm, mv, load.at[4])
    mcp.start()

    def far(steps, n):
        return min(steps, n - steps)

    xx = [xh * NXL + a] + [wrap(xh * NXL + a + i, NX) for i in range(1, NX)]
    fx = [z * (2 * NXH) + core + (v // NXL) * 2 for v in xx]
    rx0 = [(v % NXL) * NY for v in xx]
    near = sorted(((far(i, NX) + far(k, NY), i, k) for i in range(NX) for k in range(NY) if i or k), reverse=True)
    ar_xy = [(fx[i], rx0[i] + yy[k]) for _, i, k in near]
    def plane(zt, c):
        return ((zt * NXH + xh) * 2 + c, r)

    def to_planes(test, what):
        for zt in range(NZ):
            pl.when(test(zt))(functools.partial(what, zt))

    def tell(sem, d):
        pl.semaphore_signal(sem, inc=1, device_id=d, device_id_type=MESH)

    def announce(sem, zt):
        for c in range(2):
            tell(sem, plane(zt, c))

    beside = ((z * NXH + 1 - xh) * 2 + core, r)
    barrier = pltpu.get_barrier_semaphore()
    for d in (y_dev(FAR), x_dev, y_dev(1), y_dev(NY - 1), plane(z, 1 - core)):
        tell(barrier, d)

    @pl.when(xh == 0)
    def _():
        tell(barrier, beside)

    to_planes(lambda zt: zt > z, functools.partial(announce, barrier))

    def hop_out(level):
        tell(hop.at[level, 0], y_dev(1))
        tell(hop.at[level, 1], y_dev(NY - 1))

    def hop_in(level):
        pl.semaphore_wait(hop.at[level, 0], 1)
        pl.semaphore_wait(hop.at[level, 1], 1)

    def remote(s, d, ss, rs, dev):
        return pltpu.make_async_remote_copy(
            src_ref=s, dst_ref=d, send_sem=ss, recv_sem=rs, device_id=dev, device_id_type=MESH
        )

    sent = {}

    def go(s, d, flow, rs, dev):
        cp = remote(s, d, ssem.at[flow], rs, dev)
        cp.start()
        sent[flow] = sent.get(flow, 0) + 1
        return cp

    def drain(flow):
        q = pg.at[pl.ds(0, sent[flow])]
        remote(q, q, ssem.at[flow], ssem.at[flow], x_dev).wait_send()

    seen = set()

    def arrived(cp):
        if id(cp) not in seen:
            seen.add(id(cp))
            cp.wait_recv()

    def delta(d):
        rows = pl.ds(pl.multiple_of(d * SHARE, 8), SHARE)
        return fold(gv[rows, :] - lv[rows, :])

    loads[0].wait()
    loads[1].wait()
    fs[0] = delta(oth[FAR]).astype(bf)
    for k in ORDER:
        xs[k] = delta(oth[k]).astype(bf)
    pl.semaphore_wait(barrier, 5 + xh + 2 * z)

    def slot(buf, k):
        return buf.at[own[(NY - k) % NY]]

    def first(buf, flow, sems):
        return {k: go(buf.at[r], buf.at[r], flow, sems.at[k], y_dev(k)) for k in (2, 6, 1, 7)}

    def second(buf, flow, sems, got):
        arrived(got[2])
        got[3] = go(slot(buf, 2), slot(buf, 2), flow, sems.at[3], y_dev(1))
        arrived(got[6])
        got[5] = go(slot(buf, 6), slot(buf, 6), flow, sems.at[5], y_dev(7))
        s = buf.at[jnp.where(core == 0, own[6], own[2])]
        got[4] = go(s, s, flow, sems.at[4], (f, jnp.where(core == 0, own[2], own[6])))

    def pass_on(buf, flow, sems):
        q = buf.at[oth[0]]
        return [go(q, q, flow, sems.at[i], y_dev(k)) for i, k in enumerate((1, 7))]

    def over(buf, flow, sems, got, ks):
        res = {}
        for k in ks:
            if k:
                arrived(got[k])
            res[k] = go(slot(buf, k), slot(buf, k), flow, sems.at[k], x_dev)
        return res

    def send_far(i):
        return go(fs.at[i], fr.at[i], 6, far_sem.at[i], y_dev(FAR))

    hop_out(0)
    rf = [send_far(0)]
    rx = {k: go(xs.at[k], xr.at[k], 0, rxr.at[k], x_dev) for k in ORDER}
    loads[2].wait()
    loads[3].wait()
    fs[1] = delta(own[FAR]).astype(bf)
    rf.append(send_far(1))
    hop_in(0)
    hop_out(1)

    @pl.when(xh == 1)
    def _():
        tell(side, beside)

    mcp.wait()
    mg[r] = fold(mv[...]).astype(bf)
    mx = over(mg, 5, mxr, None, (0,))
    hop_in(1)
    tell(pair, x_dev)
    to_planes(lambda zt: zt < z, functools.partial(announce, up))
    ry = {}
    for k in ORDER:
        if k == ORDER[-1]:
            rf[0].wait_recv()
            xs[0] = (delta(oth[0]) + fr[0].astype(f32)).astype(bf)
            rx[0] = go(xs.at[0], xr.at[0], 0, rxr.at[0], x_dev)
        rx[k].wait_recv()
        ys[k] = (delta(own[k]) + xr[k].astype(f32)).astype(bf)
        ry[k] = go(ys.at[k], yr.at[k], 1, ryr.at[k], y_dev(k))
        if k == ORDER[2]:
            pl.semaphore_wait(pair, 1)

            @pl.when(xh == 0)
            def _():
                pl.semaphore_wait(side, 1)

            tell(both, beside)
    rf[1].wait_recv()
    total = delta(own[0]) + fr[1].astype(f32)
    for k in ORDER:
        ry[k].wait_recv()
        total = total + yr[k].astype(f32)
    rx[0].wait_recv()
    total = total + xr[0].astype(f32)
    p = total * (1.0 / REPS)
    sq = jnp.sum(p * p, axis=0, keepdims=True)
    sq = sq[:, 0:128] + sq[:, 128:256] + sq[:, 256:384] + sq[:, 384:512]
    src[0] = sq
    pl.semaphore_wait(both, 1)
    for j, d in enumerate(ar_xy):
        remote(src.at[0], arxy.at[j], asr.at[0], asr.at[1], d).start()

    pown[...] = p
    pg[r] = p.astype(bf)

    px = over(pg, 3, pxr, None, (0,))
    py = first(pg, 2, pyr)
    my = first(mg, 4, myr)
    arrived(mx[0])
    mn = pass_on(mg, 4, mnr)

    pltpu.make_async_copy(arxy, arxy, asr.at[1]).wait()
    sq = sq + jnp.sum(arxy[...], axis=0)
    src[1] = sq
    mine = 2 * z + core
    arzc[mine] = sq

    def share(zt, c):
        remote(src.at[1], arzc.at[mine], asr.at[2], asr.at[3], plane(zt, c)).start()

    def share_both(zt):
        for c in range(2):
            share(zt, c)

    def share_below(lo, hi):
        for zt in range(lo, hi):
            pl.when(zt < z)(functools.partial(share_both, zt))

    share_below(0, FIRST)
    arrived(px[0])
    pn = pass_on(pg, 2, pnr)
    second(pg, 2, pyr, py)
    px.update(over(pg, 3, pxr, py, (2, 6)))
    share_below(FIRST, NZ)
    share(z, 1 - core)

    @pl.when(z < NZ - 1)
    def _():
        pl.semaphore_wait(up, 2 * (NZ - 1 - z))

    to_planes(lambda zt: zt > z, share_both)

    second(mg, 4, myr, my)
    mx.update(over(mg, 5, mxr, my, (2, 6)))
    px.update(over(pg, 3, pxr, py, (3, 5, 4)))
    mx.update(over(mg, 5, mxr, my, (3, 5, 4)))
    for cp in [py[1], py[7], my[1], my[7]] + pn + mn + list(px.values()) + list(mx.values()):
        arrived(cp)
    for flow in range(7):
        drain(flow)
    remote(arxy, arxy, asr.at[0], asr.at[0], x_dev).wait_send()
    others = arzc.at[pl.ds(0, N_ZC)]
    remote(others, others, asr.at[2], asr.at[2], x_dev).wait_send()

    pltpu.make_async_copy(others, others, asr.at[3]).wait()
    sq = jnp.sum(arzc[...], axis=0)
    rms = jnp.sqrt(jnp.sum(sq, axis=1, keepdims=True) * (1.0 / COUNT))
    fout[...] = jnp.broadcast_to(CLIP / jnp.maximum(rms, CLIP), fout.shape)


def finish(f_ref, pown, mom, pg, mg, local, glob, new_global, new_momentum, mixed, gbuf, mbuf, xbuf, sem):
    factor = f_ref[0:1, 0:1]
    halves = [(0, pl.ds(0, HALF)), (SHARE, pl.ds(HALF, HALF))]
    cp = factor * (RATE * (1.0 + MU))
    copies = []
    per = REPS // STEPS
    for t in range(STEPS):
        for b in range(t * per, (t + 1) * per):
            rows = pl.ds(b * SHARE, SHARE)
            step = cp * pg[b].astype(jnp.float32) + (RATE * MU * MU) * mg[b].astype(jnp.float32)
            for top, cols in halves:
                updated = glob[rows, cols] - step[top:top + SHARE]
                gbuf[rows, cols] = updated
                xbuf[rows, cols] = MIXING * updated + (1.0 - MIXING) * local[rows, cols]
        rows = pl.ds(t * per * SHARE, per * SHARE)
        for i, (s, d) in enumerate(((gbuf, new_global), (xbuf, mixed))):
            q = pltpu.make_async_copy(s.at[rows], d.at[rows], sem.at[2 * t + i])
            q.start()
            copies.append(q)
    for top, cols in halves:
        mbuf[:, cols] = MU * mom[:, cols] + factor * pown[top:top + SHARE]
    q = pltpu.make_async_copy(mbuf, new_momentum, sem.at[2 * STEPS])
    q.start()
    copies.append(q)
    for q in copies:
        q.wait()


def shards(local_params, global_params, momentum):
    local = local_params[0]
    bf, f32 = jnp.bfloat16, jnp.float32
    vmem = pl.BlockSpec(memory_space=pltpu.VMEM)
    hbm = pl.BlockSpec(memory_space=pltpu.HBM)
    dma = pltpu.SemaphoreType.DMA
    gathered = jax.ShapeDtypeStruct((REPS, BLK, HALF), bf)
    in_hbm = [pltpu.with_memory_space_constraint(v, pltpu.HBM) for v in (local, global_params, momentum)]
    pg, mg, pown, factor, lv, gv, mv = pl.pallas_call(
        exchange,
        name="exchange",
        out_shape=[
            gathered,
            gathered,
            jax.ShapeDtypeStruct((BLK, HALF), f32),
            jax.ShapeDtypeStruct((8, 128), f32),
            jax.ShapeDtypeStruct((ROWS, COLS), f32),
            jax.ShapeDtypeStruct((ROWS, COLS), f32),
            jax.ShapeDtypeStruct((SHARE, COLS), f32),
        ],
        in_specs=[hbm] * 3,
        out_specs=[vmem] * 7,
        scratch_shapes=[pltpu.VMEM((NY, BLK, HALF), bf)] * 4
        + [pltpu.VMEM((2, BLK, HALF), bf)] * 2
        + [
            pltpu.VMEM((2, 1, 128), f32),
            pltpu.VMEM((N_XY, 1, 128), f32),
            pltpu.VMEM((N_ZC + 1, 1, 128), f32),
            dma((5,)),
            dma((7,)),
            dma((NY,)),
            dma((NY,)),
            dma((2,)),
            dma((NY,)),
            dma((NY,)),
            dma((2,)),
            dma((NY,)),
            dma((NY,)),
            dma((2,)),
            dma((4,)),
            pltpu.SemaphoreType.REGULAR,
            pltpu.SemaphoreType.REGULAR((2, 2)),
            pltpu.SemaphoreType.REGULAR,
            pltpu.SemaphoreType.REGULAR,
            pltpu.SemaphoreType.REGULAR,
        ],
        compiler_params=pltpu.CompilerParams(
            collective_id=0, has_side_effects=True, vmem_limit_bytes=20 << 20
        ),
    )(*in_hbm)

    any_space = pl.BlockSpec(memory_space=pl.ANY)
    new_global, new_momentum, mixed = pl.pallas_call(
        finish,
        name="finish",
        out_shape=[
            jax.ShapeDtypeStruct((ROWS, COLS), f32),
            jax.ShapeDtypeStruct((SHARE, COLS), f32),
            jax.ShapeDtypeStruct((ROWS, COLS), f32),
        ],
        in_specs=[vmem] * 7,
        out_specs=[any_space] * 3,
        scratch_shapes=[
            pltpu.VMEM((ROWS, COLS), f32),
            pltpu.VMEM((SHARE, COLS), f32),
            pltpu.VMEM((ROWS, COLS), f32),
            dma((2 * STEPS + 1,)),
        ],
        compiler_params=pltpu.CompilerParams(vmem_limit_bytes=16 << 20),
    )(factor, pown, mv, pg, mg, lv, gv)
    return (new_global, new_momentum, mixed[None])


def solution(mesh):
    placed = (P("rep", "fsdp", None), P("fsdp", None), P(("fsdp", "rep"), None))
    return jax.shard_map(
        shards,
        mesh=mesh,
        in_specs=placed,
        out_specs=(P("fsdp", None), P(("fsdp", "rep"), None), P("rep", "fsdp", None)),
        check_vma=False,
    )
```

```python
import functools

import jax
import jax.numpy as jnp
from jax import lax
from jax.experimental import pallas as pl
from jax.experimental.pallas import tpu as pltpu
from jax.sharding import PartitionSpec as P

EPS = 1e-06
CLIP = 0.3
MU = 0.9
RATE = 0.7
MIXING = 0.5

MESH = pl.DeviceIdType.MESH
NY = 8
NXL = 2
NXH = 2
NX = NXL * NXH
NZ = 12
REPS = NXL * NY
COLS = 1024
HALF = COLS // 2
SHARE = 24
BLK = 2 * SHARE
ROWS = SHARE * REPS
FIRST = 4
COUNT = float(ROWS * COLS * NZ * NXH * 2)
N_XY = NX * NY - 1
N_ZC = 2 * NZ - 1
STEPS = 4
ORDER = (3, 5, 2, 6, 1, 7)
FAR = NY // 2


def fold(v):
    return jnp.concatenate([v[:, :HALF], v[:, HALF:]], axis=0)


def exchange(
    local_hbm, global_hbm, mom_hbm,
    pg, mg, pown, fout, lv, gv, mv,
    xs, xr, ys, yr, fs, fr, src, arxy, arzc,
    load, ssem, rxr, ryr, far_sem, pyr, pxr, pnr, myr, mxr, mnr, asr, up, hop, pair, side, both,
):
    bf, f32 = jnp.bfloat16, jnp.float32
    f = lax.axis_index("fsdp")
    r = lax.axis_index("rep")
    core = f % 2
    xh = (f // 2) % NXH
    z = f // (2 * NXH)
    a = r // NY
    y = r % NY

    def wrap(t, n):
        return jnp.where(t >= n, t - n, t)

    yy = [y] + [wrap(y + k, NY) for k in range(1, NY)]
    col, ocol = a * NY, NY - a * NY
    own = [col + v for v in yy]
    oth = [ocol + v for v in yy]
    x_dev = (f, oth[0])

    def y_dev(k):
        return (f, own[k])

    loads = []
    half_rows = ROWS // NXL
    for i, c in enumerate((ocol, col)):
        rows = pl.ds(pl.multiple_of(c * SHARE, 8), half_rows)
        for j, (s, d) in enumerate(((local_hbm, lv), (global_hbm, gv))):
            cp = pltpu.make_async_copy(s.at[rows], d.at[rows], load.at[2 * i + j])
            cp.start()
            loads.append(cp)
    mcp = pltpu.make_async_copy(mom_hbm, mv, load.at[4])
    mcp.start()

    def far(steps, n):
        return min(steps, n - steps)

    xx = [xh * NXL + a] + [wrap(xh * NXL + a + i, NX) for i in range(1, NX)]
    fx = [z * (2 * NXH) + core + (v // NXL) * 2 for v in xx]
    rx0 = [(v % NXL) * NY for v in xx]
    near = sorted(((far(i, NX) + far(k, NY), i, k) for i in range(NX) for k in range(NY) if i or k), reverse=True)
    ar_xy = [(fx[i], rx0[i] + yy[k]) for _, i, k in near]
    def plane(zt, c):
        return ((zt * NXH + xh) * 2 + c, r)

    def to_planes(test, what):
        for zt in range(NZ):
            pl.when(test(zt))(functools.partial(what, zt))

    def tell(sem, d):
        pl.semaphore_signal(sem, inc=1, device_id=d, device_id_type=MESH)

    def announce(sem, zt):
        for c in range(2):
            tell(sem, plane(zt, c))

    beside = ((z * NXH + 1 - xh) * 2 + core, r)
    barrier = pltpu.get_barrier_semaphore()
    for d in (y_dev(FAR), x_dev, y_dev(1), y_dev(NY - 1), plane(z, 1 - core)):
        tell(barrier, d)

    @pl.when(xh == 0)
    def _():
        tell(barrier, beside)

    to_planes(lambda zt: zt > z, functools.partial(announce, barrier))

    def hop_out(level):
        tell(hop.at[level, 0], y_dev(1))
        tell(hop.at[level, 1], y_dev(NY - 1))

    def hop_in(level):
        pl.semaphore_wait(hop.at[level, 0], 1)
        pl.semaphore_wait(hop.at[level, 1], 1)

    def remote(s, d, ss, rs, dev):
        return pltpu.make_async_remote_copy(
            src_ref=s, dst_ref=d, send_sem=ss, recv_sem=rs, device_id=dev, device_id_type=MESH
        )

    sent = {}

    def go(s, d, flow, rs, dev, blocks=1):
        cp = remote(s, d, ssem.at[flow], rs, dev)
        cp.start()
        sent[flow] = sent.get(flow, 0) + blocks
        return cp

    def drain(flow):
        q = pg.at[pl.ds(0, sent[flow])]
        remote(q, q, ssem.at[flow], ssem.at[flow], x_dev).wait_send()

    seen = set()

    def arrived(cp):
        if id(cp) not in seen:
            seen.add(id(cp))
            cp.wait_recv()

    def delta(d):
        rows = pl.ds(pl.multiple_of(d * SHARE, 8), SHARE)
        return fold(gv[rows, :] - lv[rows, :])

    loads[0].wait()
    loads[1].wait()
    fs[0] = delta(oth[FAR]).astype(bf)
    for k in ORDER:
        xs[k] = delta(oth[k]).astype(bf)
    pl.semaphore_wait(barrier, 5 + xh + 2 * z)

    def slot(buf, k):
        return buf.at[own[(NY - k) % NY]]

    def first(buf, flow, sems):
        return {k: go(buf.at[r], buf.at[r], flow, sems.at[k], y_dev(k)) for k in (2, 6, 1, 7)}

    def second(buf, flow, sems, got):
        arrived(got[2])
        got[3] = go(slot(buf, 2), slot(buf, 2), flow, sems.at[3], y_dev(1))
        arrived(got[6])
        got[5] = go(slot(buf, 6), slot(buf, 6), flow, sems.at[5], y_dev(7))
        s = buf.at[jnp.where(core == 0, own[6], own[2])]
        got[4] = go(s, s, flow, sems.at[4], (f, jnp.where(core == 0, own[2], own[6])))

    def pass_on(buf, flow, sems):
        q = buf.at[oth[0]]
        return [go(q, q, flow, sems.at[i], y_dev(k)) for i, k in enumerate((1, 7))]

    def over(buf, flow, sems, got, ks):
        res = {}
        for k in ks:
            if k:
                arrived(got[k])
            res[k] = go(slot(buf, k), slot(buf, k), flow, sems.at[k], x_dev)
        return res

    def send_far(i):
        return go(fs.at[i], fr.at[i], 6, far_sem.at[i], y_dev(FAR))

    hop_out(0)
    rf = [send_far(0)]
    def pieces(k):
        if k not in ORDER[-2:]:
            return [(0, HALF, k, 1)]
        at = NY + 2 * ORDER[-2:].index(k)
        return [(0, HALF // 2, at, 1), (HALF // 2, HALF, at + 1, 0)]

    def send_piece(src_buf, dst_buf, k, piece, flow, sems, dev):
        lo, hi, i, n = piece
        cols = pl.ds(lo, hi - lo)
        return go(src_buf.at[k, :, cols], dst_buf.at[k, :, cols], flow, sems.at[i], dev, n)

    rx = {}
    for k in ORDER:
        for piece in pieces(k):
            rx[k, piece[2]] = send_piece(xs, xr, k, piece, 0, rxr, x_dev)
    loads[2].wait()
    loads[3].wait()
    fs[1] = delta(own[FAR]).astype(bf)
    rf.append(send_far(1))
    hop_in(0)
    hop_out(1)

    @pl.when(xh == 1)
    def _():
        tell(side, beside)

    mcp.wait()
    mg[r] = fold(mv[...]).astype(bf)
    mx = over(mg, 5, mxr, None, (0,))
    hop_in(1)
    tell(pair, x_dev)
    to_planes(lambda zt: zt < z, functools.partial(announce, up))
    ry = {}
    for k in ORDER:
        if k == ORDER[-1]:
            rf[0].wait_recv()
            xs[0] = (delta(oth[0]) + fr[0].astype(f32)).astype(bf)
            rx[0] = go(xs.at[0], xr.at[0], 0, rxr.at[0], x_dev)
        mine_k = delta(own[k])
        for piece in pieces(k):
            lo, hi, i, _ = piece
            rx[k, i].wait_recv()
            ys[k, :, lo:hi] = (mine_k[:, lo:hi] + xr[k, :, lo:hi].astype(f32)).astype(bf)
            ry[k, i] = send_piece(ys, yr, k, piece, 1, ryr, y_dev(k))
        if k == ORDER[2]:
            pl.semaphore_wait(pair, 1)

            @pl.when(xh == 0)
            def _():
                pl.semaphore_wait(side, 1)

            tell(both, beside)
    rf[1].wait_recv()
    total = delta(own[0]) + fr[1].astype(f32)
    for k in ORDER:
        for piece in pieces(k):
            ry[k, piece[2]].wait_recv()
        total = total + yr[k].astype(f32)
    rx[0].wait_recv()
    total = total + xr[0].astype(f32)
    p = total * (1.0 / REPS)
    sq = jnp.sum(p * p, axis=0, keepdims=True)
    sq = sq[:, 0:128] + sq[:, 128:256] + sq[:, 256:384] + sq[:, 384:512]
    src[0] = sq
    pl.semaphore_wait(both, 1)
    for j, d in enumerate(ar_xy):
        remote(src.at[0], arxy.at[j], asr.at[0], asr.at[1], d).start()

    pown[...] = p
    pg[r] = p.astype(bf)

    px = over(pg, 3, pxr, None, (0,))
    py = first(pg, 2, pyr)
    my = first(mg, 4, myr)
    arrived(mx[0])
    mn = pass_on(mg, 4, mnr)

    pltpu.make_async_copy(arxy, arxy, asr.at[1]).wait()
    sq = sq + jnp.sum(arxy[...], axis=0)
    src[1] = sq
    mine = 2 * z + core
    arzc[mine] = sq

    def share(zt, c):
        remote(src.at[1], arzc.at[mine], asr.at[2], asr.at[3], plane(zt, c)).start()

    def share_both(zt):
        for c in range(2):
            share(zt, c)

    def share_below(lo, hi):
        for zt in range(lo, hi):
            pl.when(zt < z)(functools.partial(share_both, zt))

    share_below(0, FIRST)
    arrived(px[0])
    pn = pass_on(pg, 2, pnr)
    second(pg, 2, pyr, py)
    px.update(over(pg, 3, pxr, py, (2, 6)))
    share_below(FIRST, NZ)
    share(z, 1 - core)

    @pl.when(z < NZ - 1)
    def _():
        pl.semaphore_wait(up, 2 * (NZ - 1 - z))

    to_planes(lambda zt: zt > z, share_both)

    second(mg, 4, myr, my)
    mx.update(over(mg, 5, mxr, my, (2, 6)))
    px.update(over(pg, 3, pxr, py, (3, 5, 4)))
    mx.update(over(mg, 5, mxr, my, (3, 5, 4)))
    for cp in [py[1], py[7], my[1], my[7]] + pn + mn + list(px.values()) + list(mx.values()):
        arrived(cp)
    for flow in range(7):
        drain(flow)
    remote(arxy, arxy, asr.at[0], asr.at[0], x_dev).wait_send()
    others = arzc.at[pl.ds(0, N_ZC)]
    remote(others, others, asr.at[2], asr.at[2], x_dev).wait_send()

    pltpu.make_async_copy(others, others, asr.at[3]).wait()
    sq = jnp.sum(arzc[...], axis=0)
    rms = jnp.sqrt(jnp.sum(sq, axis=1, keepdims=True) * (1.0 / COUNT))
    fout[...] = jnp.broadcast_to(CLIP / jnp.maximum(rms, CLIP), fout.shape)


def finish(f_ref, pown, mom, pg, mg, local, glob, new_global, new_momentum, mixed, gbuf, mbuf, xbuf, sem):
    factor = f_ref[0:1, 0:1]
    halves = [(0, pl.ds(0, HALF)), (SHARE, pl.ds(HALF, HALF))]
    cp = factor * (RATE * (1.0 + MU))
    copies = []
    per = REPS // STEPS
    for t in range(STEPS):
        for b in range(t * per, (t + 1) * per):
            rows = pl.ds(b * SHARE, SHARE)
            step = cp * pg[b].astype(jnp.float32) + (RATE * MU * MU) * mg[b].astype(jnp.float32)
            for top, cols in halves:
                updated = glob[rows, cols] - step[top:top + SHARE]
                gbuf[rows, cols] = updated
                xbuf[rows, cols] = MIXING * updated + (1.0 - MIXING) * local[rows, cols]
        rows = pl.ds(t * per * SHARE, per * SHARE)
        for i, (s, d) in enumerate(((gbuf, new_global), (xbuf, mixed))):
            q = pltpu.make_async_copy(s.at[rows], d.at[rows], sem.at[2 * t + i])
            q.start()
            copies.append(q)
    for top, cols in halves:
        mbuf[:, cols] = MU * mom[:, cols] + factor * pown[top:top + SHARE]
    q = pltpu.make_async_copy(mbuf, new_momentum, sem.at[2 * STEPS])
    q.start()
    copies.append(q)
    for q in copies:
        q.wait()


def shards(local_params, global_params, momentum):
    local = local_params[0]
    bf, f32 = jnp.bfloat16, jnp.float32
    vmem = pl.BlockSpec(memory_space=pltpu.VMEM)
    hbm = pl.BlockSpec(memory_space=pltpu.HBM)
    dma = pltpu.SemaphoreType.DMA
    gathered = jax.ShapeDtypeStruct((REPS, BLK, HALF), bf)
    in_hbm = [pltpu.with_memory_space_constraint(v, pltpu.HBM) for v in (local, global_params, momentum)]
    pg, mg, pown, factor, lv, gv, mv = pl.pallas_call(
        exchange,
        name="exchange",
        out_shape=[
            gathered,
            gathered,
            jax.ShapeDtypeStruct((BLK, HALF), f32),
            jax.ShapeDtypeStruct((8, 128), f32),
            jax.ShapeDtypeStruct((ROWS, COLS), f32),
            jax.ShapeDtypeStruct((ROWS, COLS), f32),
            jax.ShapeDtypeStruct((SHARE, COLS), f32),
        ],
        in_specs=[hbm] * 3,
        out_specs=[vmem] * 7,
        scratch_shapes=[pltpu.VMEM((NY, BLK, HALF), bf)] * 4
        + [pltpu.VMEM((2, BLK, HALF), bf)] * 2
        + [
            pltpu.VMEM((2, 1, 128), f32),
            pltpu.VMEM((N_XY, 1, 128), f32),
            pltpu.VMEM((N_ZC + 1, 1, 128), f32),
            dma((5,)),
            dma((7,)),
            dma((NY + 4,)),
            dma((NY + 4,)),
            dma((2,)),
            dma((NY,)),
            dma((NY,)),
            dma((2,)),
            dma((NY,)),
            dma((NY,)),
            dma((2,)),
            dma((4,)),
            pltpu.SemaphoreType.REGULAR,
            pltpu.SemaphoreType.REGULAR((2, 2)),
            pltpu.SemaphoreType.REGULAR,
            pltpu.SemaphoreType.REGULAR,
            pltpu.SemaphoreType.REGULAR,
        ],
        compiler_params=pltpu.CompilerParams(
            collective_id=0, has_side_effects=True, vmem_limit_bytes=20 << 20
        ),
    )(*in_hbm)

    any_space = pl.BlockSpec(memory_space=pl.ANY)
    new_global, new_momentum, mixed = pl.pallas_call(
        finish,
        name="finish",
        out_shape=[
            jax.ShapeDtypeStruct((ROWS, COLS), f32),
            jax.ShapeDtypeStruct((SHARE, COLS), f32),
            jax.ShapeDtypeStruct((ROWS, COLS), f32),
        ],
        in_specs=[vmem] * 7,
        out_specs=[any_space] * 3,
        scratch_shapes=[
            pltpu.VMEM((ROWS, COLS), f32),
            pltpu.VMEM((SHARE, COLS), f32),
            pltpu.VMEM((ROWS, COLS), f32),
            dma((2 * STEPS + 1,)),
        ],
        compiler_params=pltpu.CompilerParams(vmem_limit_bytes=16 << 20),
    )(factor, pown, mv, pg, mg, lv, gv)
    return (new_global, new_momentum, mixed[None])


def solution(mesh):
    placed = (P("rep", "fsdp", None), P("fsdp", None), P(("fsdp", "rep"), None))
    return jax.shard_map(
        shards,
        mesh=mesh,
        in_specs=placed,
        out_specs=(P("fsdp", None), P(("fsdp", "rep"), None), P("rep", "fsdp", None)),
        check_vma=False,
    )
```
